32 devices in a mesh: row: 8 (over z, x), col: 4 (over y, core).
Axes of the slice: x: 2, y: 2, z: 4, core: 2. Of those that a mesh axis runs over, the one named last changes fastest.
Arguments:
- query_sketches: bfloat16 [512, 16384], P('row', 'col'), may hold values from -200 to 200
- fisher_inverse: bfloat16 [16384, 16384], P('row', 'col'), may hold values from -1 to 3, as said below
- index_tiles: bfloat16 [4096, 16384], P('col', 'row'), may hold values from -6 to 6
Outputs:
- scores: float32 [512, 4096], P('row', 'col')
The draws below stay inside these ranges and needn't reach their ends.
Inputs may be any that keep to these rules, and one draw needn't show every extreme that they name: `fisher_inverse`: symmetric.
All inputs are finite; a program needn't handle non-finite values.
Results may differ from the reference program's by a relative error of at most 0.0029.
Values may be sent and summed in bfloat16 or wider, within the bound.
A program may use at most 64 MiB of HBM per device.

```python
import math
import jax
import jax.numpy as jnp
from jax import lax

F = 16384
QB = 512
ROWS = 4096


def draw_query_sketches(key, part):
    keys = jax.random.split(jax.random.fold_in(key, 23), 3)
    base = jnp.clip(jax.random.normal(keys[0], (QB, F), jnp.float32), -6.0, 6.0)
    scales = jnp.exp(jax.random.uniform(keys[1], (QB, 1), jnp.float32, 0.0, math.log(10.0)))
    columns = jax.random.uniform(keys[2], (1, F), jnp.float32, 0.5, 1.5)
    return jnp.clip(base * scales * columns, -200.0, 200.0).astype(jnp.bfloat16)


def draw_fisher_inverse(key, part):
    keys = jax.random.split(jax.random.fold_in(key, 11), 2)
    noise = jnp.clip(jax.random.normal(keys[0], (F, F), jnp.float32), -6.0, 6.0)
    noise = noise * F ** (-0.5)
    ramp = jnp.arange(F).astype(jnp.float32) / F
    damping = (0.5 + 1.5 * ramp) * jax.random.uniform(keys[1], (F,), jnp.float32, 0.7, 1.4)
    matrix = 0.5 * (noise + noise.T)
    places = jnp.arange(F)
    return matrix.at[places, places].add(damping).astype(jnp.bfloat16)


def block_scale(stream_key, dims, cuts, low, top_value):
    level, own = 1.0, jax.random.fold_in(stream_key, 6)
    for dim, parts in cuts:
        steps = jnp.exp(jax.random.uniform(jax.random.fold_in(own, dim), (parts,), jnp.float32, low / len(cuts), top_value / len(cuts)))
        level = level * jnp.repeat(steps, dims[dim] // parts).reshape([-1 if axis == dim else 1 for axis in range(len(dims))])
    return level


def normal_values(rng, extent, scale, limit, shards=(), dtype=jnp.bfloat16):
    drawn = jax.random.normal(rng, extent, jnp.float32) * scale
    if len(shards) > 0:
        drawn = block_scale(rng, extent, shards, -0.22, 0.18) * drawn
    return jnp.clip(drawn, min=-limit, max=limit).astype(dtype)


def setup_inputs(seed: int = 0) -> dict:
    key_of = jax.random.split(jax.random.key(seed), 4)
    return {
        "query_sketches": draw_query_sketches(jax.random.fold_in(key_of[3], 71), 0),
        "fisher_inverse": draw_fisher_inverse(jax.random.fold_in(key_of[3], 71), 0),
        "index_tiles": normal_values(key_of[2], (ROWS, F), 1.0, 6.0, ((0, 4), (1, 8))),
    }


def reference(query_sketches, fisher_inverse, index_tiles):
    preconditioned = jnp.dot(query_sketches, fisher_inverse, preferred_element_type=jnp.float32)
    squares = lax.optimization_barrier(jnp.sum(preconditioned * preconditioned, axis=1, keepdims=True))
    unit_sketch = (preconditioned / jnp.sqrt(squares + 1e-06)).astype(jnp.bfloat16)
    return jnp.dot(unit_sketch, index_tiles.T, preferred_element_type=jnp.float32)
```

```python
import functools

import jax
import jax.numpy as jnp
from jax import lax
from jax.experimental import pallas as pl
from jax.experimental.pallas import tpu as pltpu
from jax.sharding import PartitionSpec as P

NT = (((1,), (1,)), ((), ()))
Y_DTYPE = jnp.float32


def nt_dot(a, b):
    return lax.dot_general(a, b, NT, preferred_element_type=jnp.float32)


def kernel(
    line, groups, q_hbm, f_hbm, i_hbm, out_ref,
    qbuf, fbuf, ibuf, part, cbuf, half_sum, y_src, ybuf, full, keep, sx_src, sx_dst,
    sz_src, sz_dst, sq_src, sq_dst, sq_col, acc,
    load_sem, g_recv, up_send, dn_send, x_send, c1_send, c1_recv, y_send, y_recv,
    c2_send, c2_recv, sx_send, sx_recv, sz_send, sz_recv, sq_send, sq_recv,
):
    r, c = lax.axis_index("row"), lax.axis_index("col")
    z, x = r // 2, r % 2
    y, core = c // 2, c % 2
    qb, fr = qbuf.shape[2], fbuf.shape[0]
    pair, hf = 2 * qb, fr // 2
    tile = min(256, hf)
    n_row, n_col = 2 * line, 2 * groups

    load_q = pltpu.make_async_copy(q_hbm, qbuf.at[z, x], load_sem.at[0])
    load_f = pltpu.make_async_copy(f_hbm, fbuf, load_sem.at[1])
    load_i = pltpu.make_async_copy(i_hbm, ibuf, load_sem.at[2])
    load_q.start()
    load_f.start()
    load_i.start()

    def remote(src, dst, send, recv, row, col):
        return pltpu.make_async_remote_copy(
            src_ref=src, dst_ref=dst, send_sem=send, recv_sem=recv,
            device_id=(row, col), device_id_type=pl.DeviceIdType.MESH,
        )

    barrier = pltpu.get_barrier_semaphore()
    sibling = c + 1 - 2 * core
    for d in range(1, n_row):
        pl.semaphore_signal(
            barrier, inc=1, device_id=(lax.rem(r + d, n_row), c), device_id_type=pl.DeviceIdType.MESH
        )
    pl.semaphore_signal(barrier, inc=1, device_id=(r, sibling), device_id_type=pl.DeviceIdType.MESH)
    for g in range(1, groups):
        pl.semaphore_signal(
            barrier, inc=1, device_id=(r, lax.rem(c + 2 * g, n_col)), device_id_type=pl.DeviceIdType.MESH
        )
    pl.semaphore_wait(barrier, n_row - 1 + groups)

    near = jnp.minimum(z, line - 1 - z)

    def order(j):
        step = (j + 1) // 2
        close = z + step * (2 * (j % 2) - 1)
        far = jnp.where(z < line - 1 - z, j, line - 1 - j)
        return jnp.where(j <= 2 * near, close, far)

    def up_copy(zb):
        return remote(qbuf.at[zb, x], qbuf.at[zb, x], up_send.at[zb], g_recv.at[zb, x], r + 2, c)

    def dn_copy(zb):
        return remote(qbuf.at[zb, x], qbuf.at[zb, x], dn_send.at[zb], g_recv.at[zb, x], r - 2, c)

    def x_copy(zb):
        return remote(qbuf.at[zb, x], qbuf.at[zb, x], x_send.at[zb], g_recv.at[zb, x], r + 1 - 2 * x, c)

    def c1_copy(j):
        return remote(part.at[j, 1 - core], cbuf.at[j], c1_send.at[j], c1_recv.at[j], r, sibling)

    def y_copy(j, g):
        return remote(
            y_src.at[j], ybuf.at[g - 1, j], y_send.at[g - 1, j], y_recv.at[g - 1, j],
            r, lax.rem(c + 2 * g, n_col),
        )

    def c2_copy(j):
        return remote(full.at[j, core], full.at[j, core], c2_send.at[j], c2_recv.at[j], r, sibling)

    def sx_copy(j):
        return remote(sx_src.at[j], sx_dst.at[j], sx_send.at[j], sx_recv.at[j], r + 1 - 2 * x, c)

    def sz_copy(zb):
        return remote(sz_src.at[zb], sz_dst.at[z], sz_send.at[zb], sz_recv.at[z], 2 * zb + x, c)

    def sq_copy(zb, xb):
        return remote(sq_src.at[zb], sq_dst.at[z, x], sq_send.at[zb, xb], sq_recv.at[z, x], 2 * zb + xb, c)

    def forward(zb):
        x_copy(zb).start()

        @pl.when((zb <= z) & (z < line - 1))
        def _():
            up_copy(zb).start()

        @pl.when((zb >= z) & (z > 0))
        def _():
            dn_copy(zb).start()

    load_q.wait()
    forward(z)
    load_f.wait()
    load_i.wait()

    def wait_block(zb, xb):
        remote(qbuf.at[zb, xb], qbuf.at[zb, xb], x_send.at[zb], g_recv.at[zb, xb], r, c).wait_recv()

    def body(t, carry):
        @pl.when(t + 1 < line)
        def _():
            zb = order(t + 1)
            wait_block(zb, x)
            forward(zb)

        @pl.when(t < line)
        def _():
            zb = order(t)
            wait_block(zb, 1 - x)
            for h in range(2):
                @pl.loop(0, hf // tile)
                def _(n):
                    at = pl.multiple_of(n * tile, tile)
                    lhs = qbuf[zb].reshape(pair, qbuf.shape[3])
                    part[t, h, :, pl.ds(at, tile)] = nt_dot(lhs, fbuf[pl.ds(h * hf + at, tile), :])
            c1_copy(t).start()

        @pl.when((t >= 1) & (t <= line))
        def _():
            j = t - 1
            total = half_sum[j]
            for g in range(1, groups):
                y_copy(j, g).wait_recv()
                total += ybuf[g - 1, j].astype(jnp.float32)
            full[j, core] = total
            c2_copy(j).start()

        @pl.when(t < line)
        def _():
            c1_copy(t).wait_recv()
            total = part[t, core] + cbuf[t]
            half_sum[t] = total
            y_src[t] = total.astype(y_src.dtype)
            for g in range(1, groups):
                y_copy(t, g).start()

        @pl.when((t >= 1) & (t <= line))
        def _():
            j = t - 1
            zb = order(j)
            remote(
                full.at[j, 1 - core], full.at[j, 1 - core], c2_send.at[j], c2_recv.at[j], r, sibling
            ).wait_recv()
            square = jnp.zeros((8, pair), jnp.float32)
            score = jnp.zeros((pair, ibuf.shape[0]), jnp.float32)
            for h in range(2):
                p = full[j, h]
                square += lax.dot_general(
                    jnp.ones((8, hf), jnp.float32), p * p, NT,
                    preferred_element_type=jnp.float32, precision=lax.Precision.HIGHEST,
                )
                high = p.astype(jnp.bfloat16)
                low = (p - high.astype(jnp.float32)).astype(jnp.bfloat16)
                w = ibuf[:, h * hf:(h + 1) * hf]
                score += nt_dot(jnp.concatenate([high, low], axis=0), w).reshape(2, pair, -1).sum(0)
            sq_src[zb] = square
            keep[j] = score.reshape(2, qb, -1)
            sx_src[j] = keep[j, 1 - x].astype(jnp.bfloat16)
            sx_copy(j).start()
            sq_copy(zb, 1 - x).start()

            @pl.when(zb != z)
            def _():
                sq_copy(zb, x).start()

        @pl.when(t >= 2)
        def _():
            j = t - 2
            zb = order(j)
            sx_copy(j).wait_recv()
            total = keep[j, x] + sx_dst[j].astype(jnp.float32)

            @pl.when(zb == z)
            def _():
                acc[...] = total

            @pl.when(zb != z)
            def _():
                sz_src[zb] = total.astype(jnp.bfloat16)
                sz_copy(zb).start()

        return carry

    lax.fori_loop(0, line + 2, body, 0)

    def gather_squares(zb, carry):
        def one(xb):
            remote(
                sq_src.at[zb], sq_dst.at[zb, xb], sq_send.at[zb, xb], sq_recv.at[zb, xb], r, c
            ).wait_recv()
            return sq_dst[zb, xb]

        sq_col[...] += one(1 - x)

        @pl.when(zb != z)
        def _():
            sq_col[...] += one(x)
            remote(sz_src.at[zb], sz_dst.at[zb], sz_send.at[zb], sz_recv.at[zb], r, c).wait_recv()
            acc[...] += sz_dst[zb].astype(jnp.float32)

        return carry

    sq_col[...] = sq_src[z]
    lax.fori_loop(0, line, gather_squares, 0)
    scale = lax.rsqrt(sq_col[...] + 1e-06)
    column = jnp.transpose(scale)[:, :1]
    mine = jnp.where(x == 0, column[:qb], column[qb:])
    out_ref[...] = acc[...] * mine

    def drain(j, carry):
        x_copy(j).wait_send()

        @pl.when((j <= z) & (z < line - 1))
        def _():
            up_copy(j).wait_send()

        @pl.when((j >= z) & (z > 0))
        def _():
            dn_copy(j).wait_send()

        c1_copy(j).wait_send()
        for g in range(1, groups):
            y_copy(j, g).wait_send()
        c2_copy(j).wait_send()
        sx_copy(j).wait_send()
        sq_copy(j, 1 - x).wait_send()

        @pl.when(j != z)
        def _():
            sq_copy(j, x).wait_send()
            sz_copy(j).wait_send()

        return carry

    lax.fori_loop(0, line, drain, 0)


def local(n_row, n_col, q, f, i):
    line, groups = n_row // 2, n_col // 2
    qb, fc = q.shape
    fr, ib = f.shape[0], i.shape[0]
    pair, hf = 2 * qb, fr // 2
    dma = pltpu.SemaphoreType.DMA
    vm = pltpu.VMEM
    f32, bf16 = jnp.float32, jnp.bfloat16
    peers = max(groups - 1, 1)
    return pl.pallas_call(
        functools.partial(kernel, line, groups),
        out_shape=jax.ShapeDtypeStruct((qb, ib), f32),
        in_specs=[pl.BlockSpec(memory_space=pl.ANY)] * 3,
        out_specs=pl.BlockSpec(memory_space=pltpu.VMEM),
        scratch_shapes=[
            vm((line, 2, qb, fc), bf16),
            vm((fr, fc), bf16),
            vm((ib, fr), bf16),
            vm((line, 2, pair, hf), f32),
            vm((line, pair, hf), f32),
            vm((line, pair, hf), f32),
            vm((line, pair, hf), Y_DTYPE),
            vm((peers, line, pair, hf), Y_DTYPE),
            vm((line, 2, pair, hf), f32),
            vm((line, 2, qb, ib), f32),
            vm((line, qb, ib), bf16),
            vm((line, qb, ib), bf16),
            vm((line, qb, ib), bf16),
            vm((line, qb, ib), bf16),
            vm((line, 8, pair), f32),
            vm((line, 2, 8, pair), f32),
            vm((8, pair), f32),
            vm((qb, ib), f32),
            dma((3,)),
            dma((line, 2)),
            dma((line,)), dma((line,)), dma((line,)),
            dma((line,)), dma((line,)),
            dma((peers, line)), dma((peers, line)),
            dma((line,)), dma((line,)),
            dma((line,)), dma((line,)),
            dma((line,)), dma((line,)),
            dma((line, 2)), dma((line, 2)),
        ],
        compiler_params=pltpu.CompilerParams(
            collective_id=0, has_side_effects=True, vmem_limit_bytes=60 * 1024 * 1024
        ),
        cost_estimate=pl.CostEstimate(
            flops=2 * n_row * qb * fr * (fc + 2 * ib),
            bytes_accessed=2 * (fr * fc + ib * fr + qb * fc) + 4 * qb * ib,
            transcendentals=0,
        ),
    )(q, f, i)


def solution(mesh):
    placed = (P("row", "col"), P("row", "col"), P("col", "row"))
    return jax.shard_map(
        functools.partial(local, mesh.shape["row"], mesh.shape["col"]),
        mesh=mesh, in_specs=placed, out_specs=P("row", "col"), check_vma=False,
    )
```

```python
import functools

import jax
import jax.numpy as jnp
from jax import lax
from jax.experimental import pallas as pl
from jax.experimental.pallas import tpu as pltpu
from jax.sharding import PartitionSpec as P

NT = (((1,), (1,)), ((), ()))

def nt_dot(a, b):
    return lax.dot_general(a, b, NT, preferred_element_type=jnp.float32)


def kernel(
    line, groups, q_hbm, f_hbm, i_hbm, out_ref,
    qbuf, fbuf, ibuf, part, cbuf, half_sum, y_src, ybuf, ywide, full, keep, sx_src, sx_dst,
    sz_src, sz_dst, sq_src, sq_dst, sq_col, acc,
    load_sem, g_recv, up_send, dn_send, x_send, c1_send, c1_recv, y_send, y_recv,
    c2_send, c2_recv, sx_send, sx_recv, sz_send, sz_recv, sq_send, sq_recv,
):
    r, c = lax.axis_index("row"), lax.axis_index("col")
    z, x = r // 2, r % 2
    y, core = c // 2, c % 2
    qb, fr = qbuf.shape[2], fbuf.shape[0]
    pair, hf = 2 * qb, fr // 2
    tile = min(256, hf)
    n_row, n_col = 2 * line, 2 * groups

    load_q = pltpu.make_async_copy(q_hbm, qbuf.at[z, x], load_sem.at[0])
    load_f = pltpu.make_async_copy(f_hbm, fbuf, load_sem.at[1])
    load_i = pltpu.make_async_copy(i_hbm, ibuf, load_sem.at[2])
    load_q.start()
    load_f.start()
    load_i.start()

    def remote(src, dst, send, recv, row, col):
        return pltpu.make_async_remote_copy(
            src_ref=src, dst_ref=dst, send_sem=send, recv_sem=recv,
            device_id=(row, col), device_id_type=pl.DeviceIdType.MESH,
        )

    barrier = pltpu.get_barrier_semaphore()
    sibling = c + 1 - 2 * core
    for d in range(1, n_row):
        pl.semaphore_signal(
            barrier, inc=1, device_id=(lax.rem(r + d, n_row), c), device_id_type=pl.DeviceIdType.MESH
        )
    pl.semaphore_signal(barrier, inc=1, device_id=(r, sibling), device_id_type=pl.DeviceIdType.MESH)
    for g in range(1, groups):
        pl.semaphore_signal(
            barrier, inc=1, device_id=(r, lax.rem(c + 2 * g, n_col)), device_id_type=pl.DeviceIdType.MESH
        )
    pl.semaphore_wait(barrier, n_row - 1 + groups)

    near = jnp.minimum(z, line - 1 - z)

    def order(j):
        step = (j + 1) // 2
        close = z + step * (2 * (j % 2) - 1)
        far = jnp.where(z < line - 1 - z, j, line - 1 - j)
        return jnp.where(j <= 2 * near, close, far)

    def up_copy(zb):
        return remote(qbuf.at[zb, x], qbuf.at[zb, x], up_send.at[zb], g_recv.at[zb, x], r + 2, c)

    def dn_copy(zb):
        return remote(qbuf.at[zb, x], qbuf.at[zb, x], dn_send.at[zb], g_recv.at[zb, x], r - 2, c)

    def x_copy(zb):
        return remote(qbuf.at[zb, x], qbuf.at[zb, x], x_send.at[zb], g_recv.at[zb, x], r + 1 - 2 * x, c)

    def c1_copy(j):
        return remote(part.at[j, 1 - core], cbuf.at[j], c1_send.at[j], c1_recv.at[j], r, sibling)

    def y_copy(j, g):
        return remote(
            y_src.at[j], ybuf.at[g - 1, j], y_send.at[g - 1, j], y_recv.at[g - 1, j],
            r, lax.rem(c + 2 * g, n_col),
        )

    def y_wide_copy(j, g):
        return remote(
            half_sum.at[j], ywide.at[g - 1, j], y_send.at[g - 1, j], y_recv.at[g - 1, j],
            r, lax.rem(c + 2 * g, n_col),
        )

    wide = line - line // 2

    def c2_copy(j):
        return remote(full.at[j, core], full.at[j, core], c2_send.at[j], c2_recv.at[j], r, sibling)

    def sx_copy(j):
        return remote(sx_src.at[j], sx_dst.at[j], sx_send.at[j], sx_recv.at[j], r + 1 - 2 * x, c)

    def sz_copy(zb):
        return remote(sz_src.at[zb], sz_dst.at[z], sz_send.at[zb], sz_recv.at[z], 2 * zb + x, c)

    def sq_copy(zb, xb):
        return remote(sq_src.at[zb], sq_dst.at[z, x], sq_send.at[zb, xb], sq_recv.at[z, x], 2 * zb + xb, c)

    def forward(zb):
        x_copy(zb).start()

        @pl.when((zb <= z) & (z < line - 1))
        def _():
            up_copy(zb).start()

        @pl.when((zb >= z) & (z > 0))
        def _():
            dn_copy(zb).start()

    load_q.wait()
    forward(z)

    def wait_block(zb, xb):
        remote(qbuf.at[zb, xb], qbuf.at[zb, xb], x_send.at[zb], g_recv.at[zb, xb], r, c).wait_recv()

    def take(zb):
        wait_block(zb, x)
        forward(zb)

    if line > 1:
        take(order(1))
    load_f.wait()
    load_i.wait()

    def body(t, carry):
        @pl.when(t + 2 < line)
        def _():
            take(order(t + 2))

        @pl.when(t < line)
        def _():
            zb = order(t)
            wait_block(zb, 1 - x)
            for h in range(2):
                @pl.loop(0, hf // tile)
                def _(n):
                    at = pl.multiple_of(n * tile, tile)
                    lhs = qbuf[zb].reshape(pair, qbuf.shape[3])
                    part[t, h, :, pl.ds(at, tile)] = nt_dot(lhs, fbuf[pl.ds(h * hf + at, tile), :])
            c1_copy(t).start()

        @pl.when((t >= 2) & (t <= line + 1))
        def _():
            j = t - 2
            zb = order(j)
            remote(
                full.at[j, 1 - core], full.at[j, 1 - core], c2_send.at[j], c2_recv.at[j], r, sibling
            ).wait_recv()
            square = jnp.zeros((8, pair), jnp.float32)
            score = jnp.zeros((pair, ibuf.shape[0]), jnp.float32)
            for h in range(2):
                p = full[j, h]
                square += lax.dot_general(
                    jnp.ones((8, hf), jnp.float32), p * p, NT,
                    preferred_element_type=jnp.float32, precision=lax.Precision.HIGHEST,
                )
                high = p.astype(jnp.bfloat16)
                low = (p - high.astype(jnp.float32)).astype(jnp.bfloat16)
                w = ibuf[:, h * hf:(h + 1) * hf]
                score += nt_dot(jnp.concatenate([high, low], axis=0), w).reshape(2, pair, -1).sum(0)
            sq_src[zb] = square
            keep[j] = score.reshape(2, qb, -1)
            sx_src[j] = keep[j, 1 - x].astype(jnp.bfloat16)
            sx_copy(j).start()
            sq_copy(zb, 1 - x).start()

            @pl.when(zb != z)
            def _():
                sq_copy(zb, x).start()

        @pl.when(t < line)
        def _():
            c1_copy(t).wait_recv()
            total = part[t, core] + cbuf[t]
            half_sum[t] = total

            @pl.when(t < wide)
            def _():
                for g in range(1, groups):
                    y_wide_copy(t, g).start()

            @pl.when(t >= wide)
            def _():
                y_src[t] = total.astype(y_src.dtype)
                for g in range(1, groups):
                    y_copy(t, g).start()

        @pl.when((t >= 1) & (t <= line))
        def _():
            j = t - 1

            @pl.when(j < wide)
            def _():
                total = half_sum[j]
                for g in range(1, groups):
                    y_wide_copy(j, g).wait_recv()
                    total += ywide[g - 1, j]
                full[j, core] = total

            @pl.when(j >= wide)
            def _():
                total = half_sum[j]
                for g in range(1, groups):
                    y_copy(j, g).wait_recv()
                    total += ybuf[g - 1, j].astype(jnp.float32)
                full[j, core] = total

            c2_copy(j).start()

        @pl.when(t >= 3)
        def _():
            j = t - 3
            zb = order(j)
            sx_copy(j).wait_recv()
            total = keep[j, x] + sx_dst[j].astype(jnp.float32)

            @pl.when(zb == z)
            def _():
                acc[...] = total

            @pl.when(zb != z)
            def _():
                sz_src[zb] = total.astype(jnp.bfloat16)
                sz_copy(zb).start()

        return carry

    lax.fori_loop(0, line + 3, body, 0)

    def gather_squares(zb, carry):
        def one(xb):
            remote(
                sq_src.at[zb], sq_dst.at[zb, xb], sq_send.at[zb, xb], sq_recv.at[zb, xb], r, c
            ).wait_recv()
            return sq_dst[zb, xb]

        sq_col[...] += one(1 - x)

        @pl.when(zb != z)
        def _():
            sq_col[...] += one(x)
            remote(sz_src.at[zb], sz_dst.at[zb], sz_send.at[zb], sz_recv.at[zb], r, c).wait_recv()
            acc[...] += sz_dst[zb].astype(jnp.float32)

        return carry

    sq_col[...] = sq_src[z]
    lax.fori_loop(0, line, gather_squares, 0)
    scale = lax.rsqrt(sq_col[...] + 1e-06)
    column = jnp.transpose(scale)[:, :1]
    mine = jnp.where(x == 0, column[:qb], column[qb:])
    out_ref[...] = acc[...] * mine

    def drain(j, carry):
        x_copy(j).wait_send()

        @pl.when((j <= z) & (z < line - 1))
        def _():
            up_copy(j).wait_send()

        @pl.when((j >= z) & (z > 0))
        def _():
            dn_copy(j).wait_send()

        c1_copy(j).wait_send()

        @pl.when(j < wide)
        def _():
            for g in range(1, groups):
                y_wide_copy(j, g).wait_send()

        @pl.when(j >= wide)
        def _():
            for g in range(1, groups):
                y_copy(j, g).wait_send()

        c2_copy(j).wait_send()
        sx_copy(j).wait_send()
        sq_copy(j, 1 - x).wait_send()

        @pl.when(j != z)
        def _():
            sq_copy(j, x).wait_send()
            sz_copy(j).wait_send()

        return carry

    lax.fori_loop(0, line, drain, 0)


def local(n_row, n_col, q, f, i):
    line, groups = n_row // 2, n_col // 2
    qb, fc = q.shape
    fr, ib = f.shape[0], i.shape[0]
    pair, hf = 2 * qb, fr // 2
    dma = pltpu.SemaphoreType.DMA
    vm = pltpu.VMEM
    f32, bf16 = jnp.float32, jnp.bfloat16
    peers = max(groups - 1, 1)
    return pl.pallas_call(
        functools.partial(kernel, line, groups),
        out_shape=jax.ShapeDtypeStruct((qb, ib), f32),
        in_specs=[pl.BlockSpec(memory_space=pl.ANY)] * 3,
        out_specs=pl.BlockSpec(memory_space=pltpu.VMEM),
        scratch_shapes=[
            vm((line, 2, qb, fc), bf16),
            vm((fr, fc), bf16),
            vm((ib, fr), bf16),
            vm((line, 2, pair, hf), f32),
            vm((line, pair, hf), f32),
            vm((line, pair, hf), f32),
            vm((line, pair, hf), bf16),
            vm((peers, line, pair, hf), bf16),
            vm((peers, line, pair, hf), f32),
            vm((line, 2, pair, hf), f32),
            vm((line, 2, qb, ib), f32),
            vm((line, qb, ib), bf16),
            vm((line, qb, ib), bf16),
            vm((line, qb, ib), bf16),
            vm((line, qb, ib), bf16),
            vm((line, 8, pair), f32),
            vm((line, 2, 8, pair), f32),
            vm((8, pair), f32),
            vm((qb, ib), f32),
            dma((3,)),
            dma((line, 2)),
            dma((line,)), dma((line,)), dma((line,)),
            dma((line,)), dma((line,)),
            dma((peers, line)), dma((peers, line)),
            dma((line,)), dma((line,)),
            dma((line,)), dma((line,)),
            dma((line,)), dma((line,)),
            dma((line, 2)), dma((line, 2)),
        ],
        compiler_params=pltpu.CompilerParams(
            collective_id=0, has_side_effects=True, vmem_limit_bytes=60 * 1024 * 1024
        ),
        cost_estimate=pl.CostEstimate(
            flops=2 * n_row * qb * fr * (fc + 2 * ib),
            bytes_accessed=2 * (fr * fc + ib * fr + qb * fc) + 4 * qb * ib,
            transcendentals=0,
        ),
    )(q, f, i)


def solution(mesh):
    placed = (P("row", "col"), P("row", "col"), P("col", "row"))
    return jax.shard_map(
        functools.partial(local, mesh.shape["row"], mesh.shape["col"]),
        mesh=mesh, in_specs=placed, out_specs=P("row", "col"), check_vma=False,
    )
```

```python
import functools

import jax
import jax.numpy as jnp
from jax import lax
from jax.experimental import pallas as pl
from jax.experimental.pallas import tpu as pltpu
from jax.sharding import PartitionSpec as P

NT = (((1,), (1,)), ((), ()))

def nt_dot(a, b):
    return lax.dot_general(a, b, NT, preferred_element_type=jnp.float32)


def kernel(
    line, groups, q_hbm, f_hbm, i_hbm, out_ref,
    qbuf, fbuf, ibuf, part, cbuf, half_sum, y_src, ybuf, ywide, full, keep, sx_src, sx_dst,
    sz_src, sz_dst, sq_src, sq_dst, sq_col, acc,
    load_sem, g_recv, up_send, dn_send, x_send, c1_send, c1_recv, y_send, y_recv,
    c2_send, c2_recv, sx_send, sx_recv, sz_send, sz_recv, sq_send, sq_recv,
):
    r, c = lax.axis_index("row"), lax.axis_index("col")
    z, x = r // 2, r % 2
    y, core = c // 2, c % 2
    qb, fr = qbuf.shape[2], fbuf.shape[0]
    pair, hf = 2 * qb, fr // 2
    tile = min(512, hf)
    n_row, n_col = 2 * line, 2 * groups

    load_q = pltpu.make_async_copy(q_hbm, qbuf.at[z, x], load_sem.at[0])
    load_f = pltpu.make_async_copy(f_hbm, fbuf, load_sem.at[1])
    load_i = pltpu.make_async_copy(i_hbm, ibuf, load_sem.at[2])
    load_q.start()
    load_f.start()
    load_i.start()

    def remote(src, dst, send, recv, row, col):
        return pltpu.make_async_remote_copy(
            src_ref=src, dst_ref=dst, send_sem=send, recv_sem=recv,
            device_id=(row, col), device_id_type=pl.DeviceIdType.MESH,
        )

    barrier = pltpu.get_barrier_semaphore()
    sibling = c + 1 - 2 * core
    for d in range(1, n_row):
        pl.semaphore_signal(
            barrier, inc=1, device_id=(lax.rem(r + d, n_row), c), device_id_type=pl.DeviceIdType.MESH
        )
    pl.semaphore_signal(barrier, inc=1, device_id=(r, sibling), device_id_type=pl.DeviceIdType.MESH)
    for g in range(1, groups):
        pl.semaphore_signal(
            barrier, inc=1, device_id=(r, lax.rem(c + 2 * g, n_col)), device_id_type=pl.DeviceIdType.MESH
        )
    pl.semaphore_wait(barrier, n_row - 1 + groups)

    near = jnp.minimum(z, line - 1 - z)

    def order(j):
        step = (j + 1) // 2
        close = z + step * (2 * (j % 2) - 1)
        far = jnp.where(z < line - 1 - z, j, line - 1 - j)
        return jnp.where(j <= 2 * near, close, far)

    def up_copy(zb):
        return remote(qbuf.at[zb, x], qbuf.at[zb, x], up_send.at[zb], g_recv.at[zb, x], r + 2, c)

    def dn_copy(zb):
        return remote(qbuf.at[zb, x], qbuf.at[zb, x], dn_send.at[zb], g_recv.at[zb, x], r - 2, c)

    def x_copy(zb):
        return remote(qbuf.at[zb, x], qbuf.at[zb, x], x_send.at[zb], g_recv.at[zb, x], r + 1 - 2 * x, c)

    def c1_copy(j):
        return remote(part.at[j, 1 - core], cbuf.at[j], c1_send.at[j], c1_recv.at[j], r, sibling)

    def y_copy(j, g):
        return remote(
            y_src.at[j], ybuf.at[g - 1, j], y_send.at[g - 1, j], y_recv.at[g - 1, j],
            r, lax.rem(c + 2 * g, n_col),
        )

    def y_wide_copy(j, g):
        return remote(
            half_sum.at[j], ywide.at[g - 1, j], y_send.at[g - 1, j], y_recv.at[g - 1, j],
            r, lax.rem(c + 2 * g, n_col),
        )

    wide = line - line // 2

    def c2_copy(j):
        return remote(full.at[j, core], full.at[j, core], c2_send.at[j], c2_recv.at[j], r, sibling)

    def sx_copy(j):
        return remote(sx_src.at[j], sx_dst.at[j], sx_send.at[j], sx_recv.at[j], r + 1 - 2 * x, c)

    def sz_copy(zb):
        return remote(sz_src.at[zb], sz_dst.at[z], sz_send.at[zb], sz_recv.at[z], 2 * zb + x, c)

    def sq_copy(zb, xb):
        return remote(sq_src.at[zb], sq_dst.at[z, x], sq_send.at[zb, xb], sq_recv.at[z, x], 2 * zb + xb, c)

    def forward(zb):
        x_copy(zb).start()

        @pl.when((zb <= z) & (z < line - 1))
        def _():
            up_copy(zb).start()

        @pl.when((zb >= z) & (z > 0))
        def _():
            dn_copy(zb).start()

    load_q.wait()
    forward(z)

    def wait_block(zb, xb):
        remote(qbuf.at[zb, xb], qbuf.at[zb, xb], x_send.at[zb], g_recv.at[zb, xb], r, c).wait_recv()

    def take(zb):
        wait_block(zb, x)
        forward(zb)

    if line > 1:
        take(order(1))
    load_f.wait()
    load_i.wait()

    def body(t, carry):
        @pl.when(t + 2 < line)
        def _():
            take(order(t + 2))

        @pl.when(t < line)
        def _():
            zb = order(t)
            wait_block(zb, 1 - x)
            for h in (1 - core, core):
                @pl.loop(0, hf // tile)
                def _(n):
                    at = pl.multiple_of(n * tile, tile)
                    rhs = qbuf[zb].reshape(pair, qbuf.shape[3])
                    rows = pl.ds(pl.multiple_of(h * hf + at, tile), tile)
                    part[t, h, :, pl.ds(at, tile)] = nt_dot(fbuf[rows, :], rhs).T

                if h is not core:
                    c1_copy(t).start()

        @pl.when((t >= 2) & (t <= line + 1))
        def _():
            j = t - 2
            zb = order(j)
            square = jnp.zeros((8, pair), jnp.float32)
            score = jnp.zeros((pair, ibuf.shape[0]), jnp.float32)
            for h in (core, 1 - core):
                if h is not core:
                    remote(
                        full.at[j, h], full.at[j, h], c2_send.at[j], c2_recv.at[j], r, sibling
                    ).wait_recv()
                p = full[j, h]
                square += lax.dot_general(
                    jnp.ones((8, hf), jnp.float32), p * p, NT,
                    preferred_element_type=jnp.float32, precision=lax.Precision.HIGHEST,
                )
                high = p.astype(jnp.bfloat16)
                low = (p - high.astype(jnp.float32)).astype(jnp.bfloat16)
                w = ibuf[:, pl.ds(pl.multiple_of(h * hf, hf), hf)]
                score += nt_dot(jnp.concatenate([high, low], axis=0), w).reshape(2, pair, -1).sum(0)
            sq_src[zb] = square
            keep[j] = score.reshape(2, qb, -1)
            sx_src[j] = keep[j, 1 - x].astype(jnp.bfloat16)
            sx_copy(j).start()
            sq_copy(zb, 1 - x).start()

            @pl.when(zb != z)
            def _():
                sq_copy(zb, x).start()

        @pl.when(t < line)
        def _():
            c1_copy(t).wait_recv()
            total = part[t, core] + cbuf[t]
            half_sum[t] = total

            @pl.when(t < wide)
            def _():
                for g in range(1, groups):
                    y_wide_copy(t, g).start()

            @pl.when(t >= wide)
            def _():
                y_src[t] = total.astype(y_src.dtype)
                for g in range(1, groups):
                    y_copy(t, g).start()

        @pl.when((t >= 1) & (t <= line))
        def _():
            j = t - 1

            @pl.when(j < wide)
            def _():
                total = half_sum[j]
                for g in range(1, groups):
                    y_wide_copy(j, g).wait_recv()
                    total += ywide[g - 1, j]
                full[j, core] = total

            @pl.when(j >= wide)
            def _():
                total = half_sum[j]
                for g in range(1, groups):
                    y_copy(j, g).wait_recv()
                    total += ybuf[g - 1, j].astype(jnp.float32)
                full[j, core] = total

            c2_copy(j).start()

        @pl.when(t >= 3)
        def _():
            j = t - 3
            zb = order(j)
            sx_copy(j).wait_recv()
            total = keep[j, x] + sx_dst[j].astype(jnp.float32)

            @pl.when(zb == z)
            def _():
                acc[...] = total

            @pl.when(zb != z)
            def _():
                sz_src[zb] = total.astype(jnp.bfloat16)
                sz_copy(zb).start()

        return carry

    lax.fori_loop(0, line + 3, body, 0)

    def gather_squares(zb, carry):
        def one(xb):
            remote(
                sq_src.at[zb], sq_dst.at[zb, xb], sq_send.at[zb, xb], sq_recv.at[zb, xb], r, c
            ).wait_recv()
            return sq_dst[zb, xb]

        sq_col[...] += one(1 - x)

        @pl.when(zb != z)
        def _():
            sq_col[...] += one(x)
            remote(sz_src.at[zb], sz_dst.at[zb], sz_send.at[zb], sz_recv.at[zb], r, c).wait_recv()
            acc[...] += sz_dst[zb].astype(jnp.float32)

        return carry

    sq_col[...] = sq_src[z]
    lax.fori_loop(0, line, gather_squares, 0)
    scale = lax.rsqrt(sq_col[...] + 1e-06)
    column = jnp.transpose(scale)[:, :1]
    mine = jnp.where(x == 0, column[:qb], column[qb:])
    out_ref[...] = acc[...] * mine

    def drain(j, carry):
        x_copy(j).wait_send()

        @pl.when((j <= z) & (z < line - 1))
        def _():
            up_copy(j).wait_send()

        @pl.when((j >= z) & (z > 0))
        def _():
            dn_copy(j).wait_send()

        c1_copy(j).wait_send()

        @pl.when(j < wide)
        def _():
            for g in range(1, groups):
                y_wide_copy(j, g).wait_send()

        @pl.when(j >= wide)
        def _():
            for g in range(1, groups):
                y_copy(j, g).wait_send()

        c2_copy(j).wait_send()
        sx_copy(j).wait_send()
        sq_copy(j, 1 - x).wait_send()

        @pl.when(j != z)
        def _():
            sq_copy(j, x).wait_send()
            sz_copy(j).wait_send()

        return carry

    lax.fori_loop(0, line, drain, 0)


def local(n_row, n_col, q, f, i):
    line, groups = n_row // 2, n_col // 2
    qb, fc = q.shape
    fr, ib = f.shape[0], i.shape[0]
    pair, hf = 2 * qb, fr // 2
    dma = pltpu.SemaphoreType.DMA
    vm = pltpu.VMEM
    f32, bf16 = jnp.float32, jnp.bfloat16
    peers = max(groups - 1, 1)
    return pl.pallas_call(
        functools.partial(kernel, line, groups),
        out_shape=jax.ShapeDtypeStruct((qb, ib), f32),
        in_specs=[pl.BlockSpec(memory_space=pl.ANY)] * 3,
        out_specs=pl.BlockSpec(memory_space=pltpu.VMEM),
        scratch_shapes=[
            vm((line, 2, qb, fc), bf16),
            vm((fr, fc), bf16),
            vm((ib, fr), bf16),
            vm((line, 2, pair, hf), f32),
            vm((line, pair, hf), f32),
            vm((line, pair, hf), f32),
            vm((line, pair, hf), bf16),
            vm((peers, line, pair, hf), bf16),
            vm((peers, line, pair, hf), f32),
            vm((line, 2, pair, hf), f32),
            vm((line, 2, qb, ib), f32),
            vm((line, qb, ib), bf16),
            vm((line, qb, ib), bf16),
            vm((line, qb, ib), bf16),
            vm((line, qb, ib), bf16),
            vm((line, 8, pair), f32),
            vm((line, 2, 8, pair), f32),
            vm((8, pair), f32),
            vm((qb, ib), f32),
            dma((3,)),
            dma((line, 2)),
            dma((line,)), dma((line,)), dma((line,)),
            dma((line,)), dma((line,)),
            dma((peers, line)), dma((peers, line)),
            dma((line,)), dma((line,)),
            dma((line,)), dma((line,)),
            dma((line,)), dma((line,)),
            dma((line, 2)), dma((line, 2)),
        ],
        compiler_params=pltpu.CompilerParams(
            collective_id=0, has_side_effects=True, vmem_limit_bytes=60 * 1024 * 1024
        ),
        cost_estimate=pl.CostEstimate(
            flops=2 * n_row * qb * fr * (fc + 2 * ib),
            bytes_accessed=2 * (fr * fc + ib * fr + qb * fc) + 4 * qb * ib,
            transcendentals=0,
        ),
    )(q, f, i)


def solution(mesh):
    placed = (P("row", "col"), P("row", "col"), P("col", "row"))
    return jax.shard_map(
        functools.partial(local, mesh.shape["row"], mesh.shape["col"]),
        mesh=mesh, in_specs=placed, out_specs=P("row", "col"), check_vma=False,
    )
```
